128 devices in a mesh: dp: 32 (over y, z, x_hi), mp: 4 (over x_lo, core).
Axes of the slice: x: 4 (x_hi: 2, x_lo: 2; x = x_hi * 2 + x_lo), y: 4, z: 4, core: 2. Of those that a mesh axis runs over, the one named last changes fastest.
Arguments:
- student: bfloat16 [2048, 16, 1280], P('dp'), may hold values from -6 to 6
- dino_target: bfloat16 [1024, 16, 1536], P('dp', None, 'mp'), may hold values from -6 to 6
- siglip_target: bfloat16 [1024, 16, 1152], P('dp', None, 'mp'), may hold values from -6 to 6
- clip_target: bfloat16 [1024, 16, 1024], P('dp', None, 'mp'), may hold values from -6 to 6
- image_owner: int32 [1024, 1], replicated, may hold values from 0 to 31; in each aligned block of 32 rows (0 to 31, 32 to 63, ...) at most 2 rows name the same one
- patch_count: int32 [1024], replicated, may hold values from 1 to 16
- dino_expand: bfloat16 [1280, 1536], P(None, 'mp'), may hold values from -0.15625 to 0.15625
- dino_project: bfloat16 [1536, 1536], P('mp'), may hold values from -0.15625 to 0.15625
- siglip_expand: bfloat16 [1280, 1536], P(None, 'mp'), may hold values from -0.15625 to 0.15625
- siglip_project: bfloat16 [1536, 1152], P('mp'), may hold values from -0.15625 to 0.15625
- clip_expand: bfloat16 [1280, 1536], P(None, 'mp'), may hold values from -0.15625 to 0.15625
- clip_project: bfloat16 [1536, 1024], P('mp'), may hold values from -0.15625 to 0.15625
Outputs:
- student_grad: bfloat16 [2048, 16, 1280], P('dp', None, 'mp')
- dino_expand_grad: float32 [1280, 1536], P('dp', 'mp')
- dino_project_grad: float32 [1536, 1536], P('mp', 'dp')
- siglip_expand_grad: float32 [1280, 1536], P('dp', 'mp')
- siglip_project_grad: float32 [1536, 1152], P('mp', 'dp')
- clip_expand_grad: float32 [1280, 1536], P('dp', 'mp')
- clip_project_grad: float32 [1536, 1024], P('mp', 'dp')
The draws below stay inside these ranges and needn't reach their ends.
Inputs may be any that keep to these rules, and one draw needn't show every extreme that they name: `image_owner`: within each aligned block of 32 images (one store shard) no owner is named more than 2 times; every owner is named by some image.
All inputs are finite; a program needn't handle non-finite values.
Results may differ from the reference program's by a relative error of at most 0.028.
Values may be sent and summed in bfloat16 or wider, within the bound.
No kernel may reach another device: no remote copies, remote signals or barrier semaphores. Data moves between devices by JAX's collectives and lax.ppermute only.
A program may use at most 128 MiB of HBM per device.

```python
import math
import jax
import jax.numpy as jnp
import numpy as np
from jax import lax

DS = 1280
ADAPT_H = 1536
DINO_W = 1536
SIGLIP_W = 1152
CLIP_W = 1024
IMG_DEV = 32
PATCHES = 16
CAP = 2
IMAGES = 1024
SLOTS = 64
N_DP = 32
N_MP = 4


def with_ends(values, stream_key, least, largest):
    longest = values.shape.index(max(values.shape))
    spots = []
    for shift in (0, 1):
        where = [jax.random.randint(jax.random.fold_in(stream_key, axis), (), 0, length) for axis, length in enumerate(values.shape)]
        where[longest] = (where[longest] + shift) % values.shape[longest]
        spots.append(tuple(where))
    return values.at[spots[0]].set(least).at[spots[1]].set(largest)


def block_levels(key, shape, split, least, largest):
    factor_of = 1.0
    for dim, shards_of in split:
        steps = jax.random.uniform(jax.random.fold_in(jax.random.fold_in(key, 6), dim), (shards_of,), jnp.float32, least / len(split), largest / len(split))
        factor_of = factor_of * jnp.repeat(jnp.exp(steps), shape[dim] // shards_of).reshape((-1,) + (1,) * (len(shape) - 1 - dim))
    return factor_of


def deal_out(stream_key, own, number, rows, count, top, most, slope):
    ranking = jax.random.permutation(stream_key, count)
    packed, usual = load_shares(count, rows * top, most, slope, True), load_shares(count, rows * top, most, slope, False)
    places = jnp.arange(count)

    def named(tallies, rotation):
        used = int((tallies > 0).sum())
        fixed = max(1, used // 4)
        passed = fixed + (places - fixed + rotation * (used - fixed)) % max(1, count - fixed)
        return jnp.zeros((count,), jnp.int32).at[ranking[jnp.where(places < fixed, places, passed)]].set(jnp.asarray(tallies, jnp.int32))

    tallies = jnp.where(number % 4 == 0, named(packed, number // 4), named(usual, number - number // 4 - 1))
    mixed = jax.random.permutation(jax.random.fold_in(own, 3), count)
    donor, receiver = mixed[0:count // 2 * 2:2], mixed[1:count // 2 * 2:2]
    room = jnp.minimum(tallies[donor] - 1, most - tallies[receiver]) // 2
    room = jnp.where((donor == ranking[0]) | (receiver == ranking[0]) | (tallies[receiver] == 0), 0, jnp.maximum(room, 0))
    passed = jax.random.randint(jax.random.fold_in(own, 4), (count // 2,), 0, 1 << 20) % (room + 1)
    tallies = tallies.at[donor].add(-passed).at[receiver].add(passed)
    members = jnp.searchsorted(jnp.cumsum(tallies), jnp.arange(rows * top), side="right").astype(jnp.int32)
    table = members.reshape(top, rows).T
    table = table[jax.random.permutation(jax.random.fold_in(own, 1), rows)]
    rotation = jax.random.randint(jax.random.fold_in(own, 2), (rows, 1), 0, top)
    return jnp.take_along_axis(table, (jnp.arange(top)[None, :] + rotation) % top, axis=1)


def load_shares(number_of, total, bound, lean, full):
    weights = [(1 << 20) // math.isqrt(standing ** lean) + 1 for standing in range(1, number_of + 1)]
    largest = bound if full else min(bound, max(-(-total // number_of), total * weights[0] // sum(weights)))
    least = 1 if total - largest >= number_of - 1 else 0
    holding, rest = [largest] + [least] * (number_of - 1), total - largest - least * (number_of - 1)
    while rest > 0:
        free = [i for i in range(1, number_of) if holding[i] < largest] or [i for i in range(1, number_of) if holding[i] < bound]
        whole, remaining = sum([weights[i] for i in free]), rest
        for i in free:
            extra = min(bound - holding[i], max(1, remaining * weights[i] // whole), rest)
            holding[i] = holding[i] + extra
            rest = rest - extra
    return np.array(holding)


def gaussian(stream_key, extent, deviation, reach, cuts=(), held_as=jnp.bfloat16):
    array = jax.random.normal(stream_key, extent, jnp.float32) * deviation
    if len(cuts) > 0:
        array = block_levels(stream_key, extent, cuts, -0.22, 0.18) * array
    return jnp.clip(array, min=-reach, max=reach).astype(held_as)


def setup_inputs(seed: int = 0) -> dict:
    streams_of = jax.random.split(jax.random.key(seed), 13)
    student = gaussian(streams_of[0], (N_DP * SLOTS, PATCHES, DS), 1.0, 6.0, ((0, 32),))
    dino_target = gaussian(streams_of[1], (IMAGES, PATCHES, DINO_W), 1.0, 6.0, ((0, 32), (2, 4)))
    siglip_target = gaussian(streams_of[2], (IMAGES, PATCHES, SIGLIP_W), 1.0, 6.0, ((0, 32), (2, 4)))
    clip_target = gaussian(streams_of[3], (IMAGES, PATCHES, CLIP_W), 1.0, 6.0, ((0, 32), (2, 4)))
    image_owner_keys = jax.random.split(jax.random.fold_in(streams_of[4], 1), IMAGES // IMG_DEV)
    image_owner_turns = jax.random.permutation(jax.random.fold_in(streams_of[4], 3), IMAGES // IMG_DEV)
    image_owner = jax.vmap(lambda own, number: deal_out(jax.random.fold_in(streams_of[4], 2), own, number, IMG_DEV, N_DP, 1, CAP, 2))(image_owner_keys, image_owner_turns).reshape((IMAGES, 1))
    patch_count = with_ends(jax.random.randint(streams_of[5], (IMAGES,), 1, PATCHES + 1), jax.random.fold_in(streams_of[5], 1), 1, PATCHES).astype(jnp.int32)
    dino_expand = gaussian(streams_of[6], (DS, ADAPT_H), DS ** -0.5, 0.15625, ((1, 4),))
    dino_project = gaussian(streams_of[7], (ADAPT_H, DINO_W), ADAPT_H ** -0.5, 0.15625, ((0, 4),))
    siglip_expand = gaussian(streams_of[8], (DS, ADAPT_H), DS ** -0.5, 0.15625, ((1, 4),))
    siglip_project = gaussian(streams_of[9], (ADAPT_H, SIGLIP_W), ADAPT_H ** -0.5, 0.15625, ((0, 4),))
    clip_expand = gaussian(streams_of[10], (DS, ADAPT_H), DS ** -0.5, 0.15625, ((1, 4),))
    clip_project = gaussian(streams_of[11], (ADAPT_H, CLIP_W), ADAPT_H ** -0.5, 0.15625, ((0, 4),))
    return {"student": student, "dino_target": dino_target, "siglip_target": siglip_target, "clip_target": clip_target, "image_owner": image_owner, "patch_count": patch_count, "dino_expand": dino_expand, "dino_project": dino_project, "siglip_expand": siglip_expand, "siglip_project": siglip_project, "clip_expand": clip_expand, "clip_project": clip_project}


def gelu_parts(hidden):
    normal_cdf = 0.5 * (1.0 + jax.scipy.special.erf(hidden * 0.7071067811865476))
    density = jnp.exp(-0.5 * hidden * hidden) * 0.3989422804014327
    return (hidden * normal_cdf, normal_cdf + hidden * density)

def reference(student, dino_target, siglip_target, clip_target, image_owner, patch_count, dino_expand, dino_project, siglip_expand, siglip_project, clip_expand, clip_project):
    owners = image_owner[:, 0]
    store_owner = owners.reshape(N_DP, IMG_DEV)
    matching = store_owner[:, :, None] == store_owner[:, None, :]
    indices = jnp.arange(IMG_DEV, dtype=jnp.int32)
    earlier = indices[None, :] < indices[:, None]
    position = lax.optimization_barrier(jnp.sum((matching & earlier[None]).astype(jnp.int32), axis=2))
    slot = (store_owner * SLOTS + jnp.arange(N_DP, dtype=jnp.int32)[:, None] * CAP + position).reshape(-1)
    row_total = IMAGES * PATCHES
    x_rows = student[slot].reshape(row_total, DS)
    patch_index = jnp.arange(PATCHES, dtype=jnp.int32)
    valid = (patch_index[None, :] < patch_count[:, None]).astype(jnp.float32).reshape(-1)
    loss_scale = 1.0 / jnp.sqrt(jnp.sum(patch_count).astype(jnp.float32))
    group = ADAPT_H // N_MP
    partials = [jnp.zeros((row_total, DS), jnp.float32) for group_index in range(N_MP)]
    grads = []
    teachers = ((dino_target, dino_expand, dino_project), (siglip_target, siglip_expand, siglip_project), (clip_target, clip_expand, clip_project))
    for target, expand, project in teachers:
        hidden = jnp.dot(x_rows, expand, preferred_element_type=jnp.float32)
        activated, gelu_slope = gelu_parts(hidden)
        activated = activated.astype(jnp.bfloat16)
        adapted = jnp.zeros((row_total, target.shape[2]), jnp.float32)
        for group_index in range(N_MP):
            lower = group_index * group
            partial_out = jnp.dot(activated[:, lower:lower + group], project[lower:lower + group], preferred_element_type=jnp.float32).astype(jnp.bfloat16)
            adapted = adapted + lax.optimization_barrier(partial_out).astype(jnp.float32)
        target_flat = target.reshape(row_total, target.shape[2]).astype(jnp.float32)
        residual = ((adapted - target_flat) * valid[:, None]).astype(jnp.bfloat16)
        back_sum = jnp.dot(residual, project.T, preferred_element_type=jnp.float32)
        hidden_grad = (back_sum * gelu_slope).astype(jnp.bfloat16)
        grads.append(jnp.dot(x_rows.T, hidden_grad, preferred_element_type=jnp.float32) * loss_scale)
        grads.append(jnp.dot(activated.T, residual, preferred_element_type=jnp.float32) * loss_scale)
        for group_index in range(N_MP):
            lower = group_index * group
            partials[group_index] = partials[group_index] + jnp.dot(hidden_grad[:, lower:lower + group], expand[:, lower:lower + group].T, preferred_element_type=jnp.float32)
    summed = jnp.zeros((row_total, DS), jnp.float32)
    for group_index in range(N_MP):
        rounded = lax.optimization_barrier(partials[group_index].astype(jnp.bfloat16))
        summed = summed + rounded.astype(jnp.float32)
    placed = jnp.zeros((N_DP * SLOTS, PATCHES, DS), jnp.bfloat16)
    placed = placed.at[slot].set(summed.astype(jnp.bfloat16).reshape(IMAGES, PATCHES, DS))
    return (placed, grads[0], grads[1], grads[2], grads[3], grads[4], grads[5])
```

```python
import jax
import jax.numpy as jnp
from jax import lax
from jax.sharding import Mesh
from jax.sharding import PartitionSpec as P

DP = ("y", "z", "xh")
MP = ("xl", "core")
SIZES = (4, 4, 2, 2, 2)


def gelu_parts(hidden):
    normal_cdf = 0.5 * (1.0 + jax.scipy.special.erf(hidden * 0.7071067811865476))
    density = jnp.exp(-0.5 * hidden * hidden) * 0.3989422804014327
    return (hidden * normal_cdf, normal_cdf + hidden * density)


def swap(value, axis):
    return lax.ppermute(value, axis, [(0, 1), (1, 0)])


def mm(a, b, dims):
    return lax.dot_general(a, b, (dims, ((), ())), preferred_element_type=jnp.float32)


def row_plan(owners, counts, rows, core, block):
    images, patches = owners.shape[0], 16
    index = jnp.arange(images, dtype=jnp.int32)
    earlier = index[None, :] < index[:, None]
    rank = jnp.sum(((owners[:, None] == owners[None, :]) & earlier).astype(jnp.int32), axis=1)
    start = jnp.sum(jnp.where(earlier, counts[None, :], 0), axis=1)
    patch = jnp.arange(patches, dtype=jnp.int32)
    live = patch[None, :] < counts[:, None]
    number = start[:, None] + patch[None, :]
    quarter = rows // 4
    place = ((number // quarter) ^ block ^ 3) * quarter + number % quarter
    place = jnp.where(live, place, -1).reshape(-1)
    source = ((rank ^ core)[:, None] * 32 + owners[:, None]) * patches + patch[None, :]
    source = jnp.where(live, source, -1).reshape(-1)
    here = place[None, :] == jnp.arange(rows, dtype=jnp.int32)[:, None]
    origin = jnp.sum(jnp.where(here, source[None, :] + 1, 0), axis=1) - 1
    total = 2 * 32 * patches
    from_slots = origin[:, None] == jnp.arange(total, dtype=jnp.int32)[None, :]
    return here.astype(jnp.bfloat16), from_slots.astype(jnp.bfloat16)


def gather_targets(targets, core, xl, quarter):
    sent = [t[: 2 * quarter] for t in targets]
    got = swap(tuple(sent), "core")
    kept = [t[2 * quarter :] for t in targets]
    pairs = [
        jnp.concatenate([jnp.where(core == 0, k, g), jnp.where(core == 0, g, k)], axis=1)
        for k, g in zip(kept, got)
    ]
    far = swap(tuple(p[:quarter] for p in pairs), "xl")
    near = [p[quarter:] for p in pairs]
    return [
        jnp.concatenate([jnp.where(xl == 0, n, f), jnp.where(xl == 0, f, n)], axis=1)
        for n, f in zip(near, far)
    ]


def sum_over_dp(expand_grad, project_grad):
    width = project_grad.shape[0]
    e = expand_grad
    for axis in ("y", "z", "xh"):
        e = lax.psum_scatter(e, axis, scatter_dimension=0, tiled=True)
    p = project_grad.reshape(4, 4, width // 16, -1).transpose(1, 0, 2, 3)
    p = p.reshape(width, -1)
    p = lax.psum_scatter(p, "z", scatter_dimension=0, tiled=True)
    p = lax.psum_scatter(p, "y", scatter_dimension=0, tiled=True)
    p = lax.psum_scatter(p, "xh", scatter_dimension=0, tiled=True)
    return e.astype(jnp.float32), p.astype(jnp.float32).T


def step(student, targets, owners, counts, loss_scale, weights, rows):
    core, xl = lax.axis_index("core"), lax.axis_index("xl")
    block = core * 2 + xl
    quarter = rows // 4
    half = rows // 2
    to_rows, from_slots = row_plan(owners, counts, rows, core, block)

    slots = student.reshape(32, 2, 16, -1)
    mine = lax.dynamic_index_in_dim(slots, core, 1, keepdims=False)
    mine = lax.all_to_all(mine, DP, split_axis=0, concat_axis=0, tiled=True)
    mine = mine.reshape(32 * 16, -1)
    other = swap(mine, "core")
    x = (mm(from_slots[:, :512], mine, ((1,), (0,))) + mm(from_slots[:, 512:], other, ((1,), (0,)))).astype(jnp.bfloat16)

    compact = [
        mm(to_rows, t.reshape(512, -1), ((1,), (0,))).astype(jnp.bfloat16) for t in targets
    ]
    wanted = gather_targets(compact, core, xl, quarter)

    acts, slopes, residuals = [], [], []
    for (expand, project), target in zip(weights, wanted):
        hidden = mm(x, expand, ((1,), (0,)))
        act, slope = gelu_parts(hidden)
        act = act.astype(jnp.bfloat16)
        near = swap(mm(act[:half], project, ((1,), (0,))).astype(jnp.bfloat16), "core")
        far_sum = mm(act[half : half + quarter], project, ((1,), (0,))) + near[:quarter].astype(jnp.float32)
        far = swap(far_sum.astype(jnp.bfloat16), "xl")
        own = mm(act[half + quarter :], project, ((1,), (0,))) + near[quarter:].astype(jnp.float32)
        residual = (own + far.astype(jnp.float32)) - target.astype(jnp.float32)
        acts.append(act)
        slopes.append(slope)
        residuals.append(residual.astype(jnp.bfloat16))

    results, hidden_grads = [], []
    for (expand, project), act, slope, own in zip(weights, acts, slopes, residuals):
        by_core = swap(own, "core")
        by_xl = swap(own, "xl")
        by_both = swap(by_xl, "core")
        residual = jnp.concatenate([by_both, by_core, by_xl, own], axis=0)
        project_grad = (mm(residual, act, ((0,), (0,))) * loss_scale).astype(jnp.bfloat16)
        back = mm(residual, project, ((1,), (1,)))
        hidden_grad = (back * slope).astype(jnp.bfloat16)
        expand_grad = (mm(x, hidden_grad, ((0,), (0,))) * loss_scale).astype(jnp.bfloat16)
        results.extend(sum_over_dp(expand_grad, project_grad))
        hidden_grads.append(hidden_grad)

    def columns(xl_of, core_of):
        start = (xl_of * 2 + core_of) * 320
        total = 0.0
        for (expand, _), hidden_grad in zip(weights, hidden_grads):
            part = lax.dynamic_slice_in_dim(expand, start, 320, 0)
            total = total + mm(hidden_grad, part, ((1,), (1,)))
        return total

    def core_order(value):
        return jnp.concatenate([value[half:], value[:half]], axis=0)

    def xl_order(value):
        cuts = [value[i * quarter : (i + 1) * quarter] for i in range(4)]
        return jnp.concatenate([cuts[1], cuts[0], cuts[3], cuts[2]], axis=0)

    near_far = swap(columns(1 - xl, 1 - core).astype(jnp.bfloat16), "core")
    near_own = swap(columns(xl, 1 - core).astype(jnp.bfloat16), "core")
    far = swap(
        (columns(1 - xl, core) + core_order(near_far).astype(jnp.float32)).astype(jnp.bfloat16), "xl"
    )
    own = columns(xl, core) + core_order(near_own).astype(jnp.float32)
    grad = (own + xl_order(far).astype(jnp.float32)).astype(jnp.bfloat16)
    placed = mm(from_slots, grad, ((0,), (0,))).astype(jnp.bfloat16).reshape(2, 32, 16, -1)
    placed = jnp.where(core == 0, placed, placed[::-1]).transpose(1, 0, 2, 3)
    sent = lax.all_to_all(placed, DP, split_axis=0, concat_axis=0, tiled=True)
    return (sent.reshape(student.shape[0], 16, -1), *results)


def shards(
    student,
    dino_target,
    siglip_target,
    clip_target,
    image_owner,
    patch_count,
    dino_expand,
    dino_project,
    siglip_expand,
    siglip_project,
    clip_expand,
    clip_project,
):
    store = (lax.axis_index("y") * 4 + lax.axis_index("z")) * 2 + lax.axis_index("xh")
    per_store = dino_target.shape[0]
    owners = lax.dynamic_slice_in_dim(image_owner[:, 0], store * per_store, per_store)
    counts = lax.dynamic_slice_in_dim(patch_count, store * per_store, per_store)
    loss_scale = 1.0 / jnp.sqrt(jnp.sum(patch_count).astype(jnp.float32))
    weights = (
        (dino_expand, dino_project),
        (siglip_expand, siglip_project),
        (clip_expand, clip_project),
    )
    return step(
        student, (dino_target, siglip_target, clip_target), owners, counts, loss_scale, weights, 512
    )


def solution(mesh):
    fine = Mesh(mesh.devices.reshape(SIZES), DP + MP)
    return jax.shard_map(
        shards,
        mesh=fine,
        in_specs=(
            P(DP, None, None),
            P(DP, None, MP),
            P(DP, None, MP),
            P(DP, None, MP),
            P(),
            P(),
            P(None, MP),
            P(MP, None),
            P(None, MP),
            P(MP, None),
            P(None, MP),
            P(MP, None),
        ),
        out_specs=(
            P(DP, None, MP),
            P(DP, MP),
            P(MP, DP),
            P(DP, MP),
            P(MP, DP),
            P(DP, MP),
            P(MP, DP),
        ),
        check_vma=False,
    )
```

```python
import jax
import jax.numpy as jnp
from jax import lax
from jax.sharding import Mesh
from jax.sharding import PartitionSpec as P

DP = ("y", "z", "xh")
MP = ("xl", "core")
SIZES = (4, 4, 2, 2, 2)


def gelu_parts(hidden):
    normal_cdf = 0.5 * (1.0 + jax.scipy.special.erf(hidden * 0.7071067811865476))
    density = jnp.exp(-0.5 * hidden * hidden) * 0.3989422804014327
    return (hidden * normal_cdf, normal_cdf + hidden * density)


def swap(value, axis):
    return lax.ppermute(value, axis, [(0, 1), (1, 0)])


def mm(a, b, dims):
    return lax.dot_general(a, b, (dims, ((), ())), preferred_element_type=jnp.float32)


def row_plan(owners, counts, rows, core):
    images, patches = owners.shape[0], 16
    index = jnp.arange(images, dtype=jnp.int32)
    earlier = index[None, :] < index[:, None]
    rank = jnp.sum(((owners[:, None] == owners[None, :]) & earlier).astype(jnp.int32), axis=1)
    start = jnp.sum(jnp.where(earlier, counts[None, :], 0), axis=1)
    patch = jnp.arange(patches, dtype=jnp.int32)
    live = patch[None, :] < counts[:, None]
    number = start[:, None] + patch[None, :]
    half = rows // 2
    upper = (number >= half).astype(jnp.int32)
    place = number - upper * half + (upper ^ core ^ 1) * half
    place = jnp.where(live, place, -1).reshape(-1)
    source = ((rank ^ core)[:, None] * 32 + owners[:, None]) * patches + patch[None, :]
    source = jnp.where(live, source, -1).reshape(-1)
    here = place[None, :] == jnp.arange(rows, dtype=jnp.int32)[:, None]
    origin = jnp.sum(jnp.where(here, source[None, :] + 1, 0), axis=1) - 1
    total = 2 * 32 * patches
    from_slots = origin[:, None] == jnp.arange(total, dtype=jnp.int32)[None, :]
    return here.astype(jnp.bfloat16), from_slots.astype(jnp.bfloat16)


def after(value, *others):
    return lax.optimization_barrier((value, others))[0]


def ring_cuts(parts, axis, dim, flip=0):
    here = lax.axis_index(axis)

    def cut(ahead):
        index = ((here + ahead) % 4) ^ flip
        cuts = [lax.dynamic_index_in_dim(value, index, dim, keepdims=False) for value in parts]
        return cuts[0] if len(cuts) == 1 else jnp.concatenate(cuts, axis=-2)

    return [cut(ahead) for ahead in range(4)]


def ring_send(cuts, axis):
    return [cuts[0]] + [
        lax.ppermute(cuts[ahead], axis, [(i, (i + ahead) % 4) for i in range(4)])
        for ahead in (1, 3, 2)
    ]


def ring_add(arrived):
    total = arrived[0].astype(jnp.float32)
    for value in arrived[1:]:
        total = total + value.astype(jnp.float32)
    return total.astype(jnp.bfloat16)


def first_cuts(pairs):
    flip = lax.axis_index("xl") * 2
    expand = ring_cuts([e.reshape(4, 4, -1, 384) for e, _ in pairs], "z", 1)
    project = ring_cuts([p.reshape(4, 4, -1, 384) for _, p in pairs], "y", 0, flip)
    return expand, project


def first_phase(cuts):
    return ring_add(ring_send(cuts[0], "z")), ring_add(ring_send(cuts[1], "y"))


def second_phase(groups):
    expand = ring_cuts([e for e, _ in groups], "y", 0)
    project = ring_cuts([p for _, p in groups], "z", 0)
    return ring_add(ring_send(expand, "y")), ring_add(ring_send(project, "z"))


def third_phase(expand, project, widths):
    xh = lax.axis_index("xh")
    lows, highs = [], []
    for whole, rows in ((expand, [40] * len(widths)), (project, [w // 32 for w in widths])):
        at = 0
        for n in rows:
            lows.append(whole[at : at + n])
            highs.append(whole[at + n : at + 2 * n])
            at += 2 * n
    low, high = jnp.concatenate(lows, axis=0), jnp.concatenate(highs, axis=0)
    got = swap(jnp.where(xh == 0, high, low), "xh")
    total = jnp.where(xh == 0, low, high).astype(jnp.float32) + got.astype(jnp.float32)
    at, outs = 0, []
    for value in lows:
        outs.append(total[at : at + value.shape[0]])
        at += value.shape[0]
    n = len(widths)
    return [(outs[i], outs[n + i].T) for i in range(n)]


def step(student, targets, owners, counts, loss_scale, weights, rows):
    core, xl = lax.axis_index("core"), lax.axis_index("xl")
    half = rows // 2

    slots = student.reshape(32, 2, 16, -1)
    mine = lax.dynamic_index_in_dim(slots, core, 1, keepdims=False)
    mine = lax.all_to_all(mine, DP, split_axis=0, concat_axis=0, tiled=True)
    mine = mine.reshape(32 * 16, -1)
    other = swap(mine, "core")
    to_rows, from_slots = row_plan(owners, counts, rows, core)
    x = (
        mm(from_slots[:, :512], mine, ((1,), (0,))) + mm(from_slots[:, 512:], other, ((1,), (0,)))
    ).astype(jnp.bfloat16)

    def halves(project):
        cut = project.shape[1] // 2
        low, high = project[:, :cut], project[:, cut:]
        return jnp.where(xl == 0, low, high), jnp.where(xl == 0, high, low)

    acts, slopes, cuts = [], [], []
    for expand, project in weights:
        act, slope = gelu_parts(mm(x, expand, ((1,), (0,))))
        acts.append(act.astype(jnp.bfloat16))
        slopes.append(slope)
        cuts.append(halves(project))

    far_sums, nears = [], []
    for i, (own_cut, far_cut) in enumerate(cuts):
        if i > 0:
            acts[i] = after(acts[i], far_sums[-1])
        act = acts[i]
        near_far = swap(mm(act[:half], far_cut, ((1,), (0,))).astype(jnp.bfloat16), "core")
        nears.append(swap(mm(act[:half], own_cut, ((1,), (0,))).astype(jnp.bfloat16), "core"))
        far_sum = mm(act[half:], far_cut, ((1,), (0,))) + near_far.astype(jnp.float32)
        far_sums.append(far_sum.astype(jnp.bfloat16))
    targets = after(targets, far_sums[0])

    wanted = []
    for target in targets:
        flat = target.reshape(512, -1)
        sent = mm(to_rows[:half], flat, ((1,), (0,))).astype(jnp.bfloat16)
        kept = mm(to_rows[half:], flat, ((1,), (0,))).astype(jnp.bfloat16)
        got = swap(sent, "core")
        wanted.append(
            jnp.concatenate([jnp.where(core == 0, kept, got), jnp.where(core == 0, got, kept)], axis=1)
        )

    owns = []
    for (own_cut, _), act, near_own, target in zip(cuts, acts, nears, wanted):
        own = mm(after(act[half:], far_sums[2]), own_cut, ((1,), (0,)))
        owns.append((own + near_own.astype(jnp.float32)) - target.astype(jnp.float32))
    by_xl, by_core, residuals = [], [], []
    for i, (own, far_sum) in enumerate(zip(owns, far_sums)):
        if i > 0:
            own = after(own, residuals[-1])
        residual = (own + swap(far_sum, "xl").astype(jnp.float32)).astype(jnp.bfloat16)
        residuals.append(residual)
        by_xl.append(swap(residual, "xl"))
        by_core.append(swap(residual, "core"))

    pairs, hidden_grads, waiting = [], [], []
    for i, (own_cut, far_cut) in enumerate(cuts):
        act, slope = acts[i], slopes[i]
        if i > 0:
            by_xl[i] = after(by_xl[i], pairs[-1] if i == 2 else waiting[-1])
        near = jnp.concatenate([by_core[i], residuals[i]], axis=0)
        far = jnp.concatenate([swap(by_xl[i], "core"), by_xl[i]], axis=0)
        back = mm(near, own_cut, ((1,), (1,))) + mm(far, far_cut, ((1,), (1,)))
        hidden_grad = (back * slope).astype(jnp.bfloat16)
        project_grad = jnp.concatenate(
            [
                (mm(part, act, ((0,), (0,))) * loss_scale).astype(jnp.bfloat16)
                for part in (near, far)
            ],
            axis=0,
        )
        expand_grad = (mm(x, hidden_grad, ((0,), (0,))) * loss_scale).astype(jnp.bfloat16)
        pairs.append((expand_grad, project_grad))
        hidden_grads.append(hidden_grad)
        if i == 0:
            waiting.append(first_cuts(pairs))

    def columns(xl_of, core_of):
        start = (xl_of * 2 + core_of) * 320
        total = 0.0
        for (expand, _), hidden_grad in zip(weights, hidden_grads):
            part = lax.dynamic_slice_in_dim(expand, start, 320, 0)
            total = total + mm(hidden_grad, part, ((1,), (1,)))
        return total

    def core_order(value):
        return jnp.concatenate([value[half:], value[:half]], axis=0).astype(jnp.float32)

    near_far = columns(1 - xl, 1 - core).astype(jnp.bfloat16)
    near_own = columns(xl, 1 - core).astype(jnp.bfloat16)
    near_far, near_own = swap(near_far, "core"), swap(near_own, "core")
    far_sum = (columns(1 - xl, core) + core_order(near_far)).astype(jnp.bfloat16)
    far = swap(far_sum, "xl")
    waiting.append(first_cuts(after(pairs[1:], far_sum)))
    groups = [first_phase(cuts) for cuts in waiting]
    own = columns(xl, core) + core_order(near_own)
    grad = (own + far.astype(jnp.float32)).astype(jnp.bfloat16)
    placed = mm(from_slots, grad, ((0,), (0,))).astype(jnp.bfloat16).reshape(2, 32, 16, -1)
    placed = jnp.where(core == 0, placed, placed[::-1]).transpose(1, 0, 2, 3)
    sent = lax.all_to_all(placed, DP, split_axis=0, concat_axis=0, tiled=True)
    sums = second_phase(after(groups, placed))
    sums = after(sums, sent)
    sums = third_phase(*sums, [project.shape[1] for _, project in weights])
    results = [value for pair in sums for value in pair]
    return (sent.reshape(student.shape[0], 16, -1), *results)


def shards(
    student,
    dino_target,
    siglip_target,
    clip_target,
    image_owner,
    patch_count,
    dino_expand,
    dino_project,
    siglip_expand,
    siglip_project,
    clip_expand,
    clip_project,
):
    store = (lax.axis_index("y") * 4 + lax.axis_index("z")) * 2 + lax.axis_index("xh")
    per_store = dino_target.shape[0]
    owners = lax.dynamic_slice_in_dim(image_owner[:, 0], store * per_store, per_store)
    counts = lax.dynamic_slice_in_dim(patch_count, store * per_store, per_store)
    loss_scale = 1.0 / jnp.sqrt(jnp.sum(patch_count).astype(jnp.float32))
    weights = (
        (dino_expand, dino_project),
        (siglip_expand, siglip_project),
        (clip_expand, clip_project),
    )
    return step(
        student, (dino_target, siglip_target, clip_target), owners, counts, loss_scale, weights, 512
    )


def solution(mesh):
    fine = Mesh(mesh.devices.reshape(SIZES), DP + MP)
    return jax.shard_map(
        shards,
        mesh=fine,
        in_specs=(
            P(DP, None, None),
            P(DP, None, MP),
            P(DP, None, MP),
            P(DP, None, MP),
            P(),
            P(),
            P(None, MP),
            P(MP, None),
            P(None, MP),
            P(MP, None),
            P(None, MP),
            P(MP, None),
        ),
        out_specs=(
            P(DP, None, MP),
            P(DP, MP),
            P(MP, DP),
            P(DP, MP),
            P(MP, DP),
            P(DP, MP),
            P(MP, DP),
        ),
        check_vma=False,
    )
```

```python
import jax
import jax.numpy as jnp
from jax import lax
from jax.sharding import Mesh
from jax.sharding import PartitionSpec as P

DP = ("y", "z", "xh")
MP = ("xl", "core")
SIZES = (4, 4, 2, 2, 2)


def gelu_parts(hidden):
    normal_cdf = 0.5 * (1.0 + jax.scipy.special.erf(hidden * 0.7071067811865476))
    density = jnp.exp(-0.5 * hidden * hidden) * 0.3989422804014327
    return (hidden * normal_cdf, normal_cdf + hidden * density)


def swap(value, axis):
    return lax.ppermute(value, axis, [(0, 1), (1, 0)])


def mm(a, b, dims):
    return lax.dot_general(a, b, (dims, ((), ())), preferred_element_type=jnp.float32)


def row_plan(owners, counts, rows, core):
    images, patches = owners.shape[0], 16
    index = jnp.arange(images, dtype=jnp.int32)
    earlier = index[None, :] < index[:, None]
    rank = jnp.sum(((owners[:, None] == owners[None, :]) & earlier).astype(jnp.int32), axis=1)
    start = jnp.sum(jnp.where(earlier, counts[None, :], 0), axis=1)
    patch = jnp.arange(patches, dtype=jnp.int32)
    live = patch[None, :] < counts[:, None]
    number = start[:, None] + patch[None, :]
    half = rows // 2
    upper = (number >= half).astype(jnp.int32)
    place = number - upper * half + (upper ^ core ^ 1) * half
    place = jnp.where(live, place, -1).reshape(-1)
    source = ((rank ^ core)[:, None] * 32 + owners[:, None]) * patches + patch[None, :]
    source = jnp.where(live, source, -1).reshape(-1)
    here = place[None, :] == jnp.arange(rows, dtype=jnp.int32)[:, None]
    origin = jnp.sum(jnp.where(here, source[None, :] + 1, 0), axis=1) - 1
    total = 2 * 32 * patches
    from_slots = origin[:, None] == jnp.arange(total, dtype=jnp.int32)[None, :]
    return here.astype(jnp.bfloat16), from_slots.astype(jnp.bfloat16)


def after(value, *others):
    return lax.optimization_barrier((value, others))[0]


def ring_cuts(parts, axis, dim, flip=0):
    here = lax.axis_index(axis)

    def cut(ahead):
        index = ((here + ahead) % 4) ^ flip
        cuts = [lax.dynamic_index_in_dim(value, index, dim, keepdims=False) for value in parts]
        return cuts[0] if len(cuts) == 1 else jnp.concatenate(cuts, axis=-2)

    return [cut(ahead) for ahead in range(4)]


def ring_send(cuts, axis):
    return [cuts[0]] + [
        lax.ppermute(cuts[ahead], axis, [(i, (i + ahead) % 4) for i in range(4)])
        for ahead in (1, 3, 2)
    ]


def ring_add(arrived):
    total = arrived[0].astype(jnp.float32)
    for value in arrived[1:]:
        total = total + value.astype(jnp.float32)
    return total.astype(jnp.bfloat16)


def ring_ask(parts, axis, dim, flip=0):
    chunks = ring_cuts(parts, axis, dim, flip)
    return chunks, (chunks[2][:2], chunks[2][2:])


def ring_first(halves, axis):
    ahead, behind = [(i, (i + 1) % 4) for i in range(4)], [(i, (i + 3) % 4) for i in range(4)]
    return lax.ppermute(halves[0], axis, ahead), lax.ppermute(halves[1], axis, behind)


def ring_next(chunks, arrived):
    up = chunks[1][:2].astype(jnp.float32) + arrived[0].astype(jnp.float32)
    down = chunks[3][2:].astype(jnp.float32) + arrived[1].astype(jnp.float32)
    return (
        jnp.concatenate([up.astype(jnp.bfloat16), chunks[1][2:]], axis=0),
        jnp.concatenate([chunks[3][:2], down.astype(jnp.bfloat16)], axis=0),
    )


def second_phase(expand, project):
    expand = ring_cuts([expand], "y", 0)
    project = ring_cuts([project], "z", 0)
    return ring_add(ring_send(expand, "y")), ring_add(ring_send(project, "z"))


def third_phase(expand, project, widths):
    xh = lax.axis_index("xh")

    def add(low, high):
        got = swap(jnp.where(xh == 0, high, low), "xh")
        return jnp.where(xh == 0, low, high).astype(jnp.float32) + got.astype(jnp.float32)

    at, cuts = 0, []
    for width in widths:
        cuts.append(project[at : at + width // 16])
        at += width // 16
    low = jnp.concatenate([cut[: cut.shape[0] // 2] for cut in cuts], axis=0)
    high = jnp.concatenate([cut[cut.shape[0] // 2 :] for cut in cuts], axis=0)
    second = add(low, high)
    first = add(expand[:40], expand[40:])
    at, outs = 0, []
    for i, width in enumerate(widths):
        rows = width // 32
        outs.append((first[:, 384 * i : 384 * (i + 1)], second[at : at + rows].T))
        at += rows
    return outs


def step(student, targets, owners, counts, loss_scale, weights, rows):
    core, xl = lax.axis_index("core"), lax.axis_index("xl")
    half = rows // 2

    slots = student.reshape(32, 2, 16, -1)
    mine = lax.dynamic_index_in_dim(slots, core, 1, keepdims=False)
    mine = lax.all_to_all(mine, DP, split_axis=0, concat_axis=0, tiled=True)
    mine = mine.reshape(32 * 16, -1)

    def halves(project):
        cut = project.shape[1] // 2
        low, high = project[:, :cut], project[:, cut:]
        return jnp.where(xl == 0, low, high), jnp.where(xl == 0, high, low)
    expands = jnp.concatenate([expand for expand, _ in weights], axis=1)
    cuts = [halves(project) for _, project in weights]
    to_rows, from_slots = row_plan(owners, counts, rows, core)
    mine = after(mine, expands, cuts, from_slots)
    other = swap(mine, "core")
    x = (
        mm(from_slots[:, :512], mine, ((1,), (0,))) + mm(from_slots[:, 512:], other, ((1,), (0,)))
    ).astype(jnp.bfloat16)

    act_all, slope_all = gelu_parts(mm(x, expands, ((1,), (0,))))
    act_all = act_all.astype(jnp.bfloat16)
    acts = [act_all[:, 384 * i : 384 * (i + 1)] for i in range(3)]

    far_sums, nears = [], []
    for i, (own_cut, far_cut) in enumerate(cuts):
        if i > 0:
            acts[i] = after(acts[i], far_sums[-1])
        act = acts[i]
        near_far = swap(mm(act[:half], far_cut, ((1,), (0,))).astype(jnp.bfloat16), "core")
        nears.append(swap(mm(act[:half], own_cut, ((1,), (0,))).astype(jnp.bfloat16), "core"))
        far_sum = mm(act[half:], far_cut, ((1,), (0,))) + near_far.astype(jnp.float32)
        far_sums.append(far_sum.astype(jnp.bfloat16))
    targets = after(targets, far_sums[0])

    wanted = []
    for target in targets:
        flat = target.reshape(512, -1)
        sent = mm(to_rows[:half], flat, ((1,), (0,))).astype(jnp.bfloat16)
        kept = mm(to_rows[half:], flat, ((1,), (0,))).astype(jnp.bfloat16)
        got = swap(sent, "core")
        wanted.append(
            jnp.concatenate([jnp.where(core == 0, kept, got), jnp.where(core == 0, got, kept)], axis=1)
        )

    owns = []
    for (own_cut, _), act, near_own, target in zip(cuts, acts, nears, wanted):
        own = mm(after(act[half:], far_sums[2]), own_cut, ((1,), (0,)))
        owns.append((own + near_own.astype(jnp.float32)) - target.astype(jnp.float32))
    by_xl, by_core, residuals = [], [], []
    for i, (own, far_sum) in enumerate(zip(owns, far_sums)):
        if i > 0:
            own = after(own, residuals[-1])
        residual = (own + swap(far_sum, "xl").astype(jnp.float32)).astype(jnp.bfloat16)
        residuals.append(residual)
        by_xl.append(swap(residual, "xl"))
        by_core.append(swap(residual, "core"))

    flip = xl * 2
    blocks, project_grads = [], []
    for i in range(3):
        act = act_all[:, 384 * i : 384 * (i + 1)]
        near = jnp.concatenate([by_core[i], residuals[i]], axis=0)
        far = jnp.concatenate([swap(by_xl[i], "core"), by_xl[i]], axis=0)
        blocks.append((near, far))
        parts = [mm(part, act, ((0,), (0,))) * loss_scale for part in (near, far)]
        project_grads.append(jnp.concatenate([p.astype(jnp.bfloat16) for p in parts], axis=0))
    project_chunks, project_halves = ring_ask(
        [p.reshape(4, 4, -1, 384) for p in project_grads], "y", 0, flip
    )
    project_came = ring_first(project_halves, "y")
    blocks = after(blocks, project_halves)
    backs = [
        mm(near, own_cut, ((1,), (1,))) + mm(far, far_cut, ((1,), (1,)))
        for (near, far), (own_cut, far_cut) in zip(blocks, cuts)
    ]
    hidden_grad = (jnp.concatenate(backs, axis=1) * slope_all).astype(jnp.bfloat16)
    expand_grad = (mm(x, hidden_grad, ((0,), (0,))) * loss_scale).astype(jnp.bfloat16)
    expand_chunks, expand_halves = ring_ask([expand_grad.reshape(4, 4, 80, -1)], "z", 1)
    expand_came = ring_first(expand_halves, "z")
    hidden_grad = after(hidden_grad, expand_halves)

    def columns(xl_of, core_of):
        part = lax.dynamic_slice_in_dim(expands, (xl_of * 2 + core_of) * 320, 320, 0)
        return mm(hidden_grad, part, ((1,), (1,)))

    def core_order(value):
        return jnp.concatenate([value[half:], value[:half]], axis=0).astype(jnp.float32)

    near_far = columns(1 - xl, 1 - core).astype(jnp.bfloat16)
    near_own = columns(xl, 1 - core).astype(jnp.bfloat16)
    near_far, near_own = swap(near_far, "core"), swap(near_own, "core")
    far_sum = (columns(1 - xl, core) + core_order(near_far)).astype(jnp.bfloat16)
    far = swap(far_sum, "xl")
    project_next = ring_next(after(project_chunks, far_sum), project_came)
    expand_next = ring_next(after(expand_chunks, far_sum), expand_came)
    project_sums = ring_first(project_next, "y")
    expand_sums = ring_first(expand_next, "z")
    own = columns(xl, core) + core_order(near_own)
    grad = (own + far.astype(jnp.float32)).astype(jnp.bfloat16)
    placed = mm(from_slots, grad, ((0,), (0,))).astype(jnp.bfloat16).reshape(2, 32, 16, -1)
    placed = jnp.where(core == 0, placed, placed[::-1]).transpose(1, 0, 2, 3)
    sent = lax.all_to_all(placed, DP, split_axis=0, concat_axis=0, tiled=True)
    sums = second_phase(
        ring_add([after(expand_chunks[0], placed), *expand_sums]),
        ring_add([after(project_chunks[0], placed), *project_sums]),
    )
    sums = after(sums, sent)
    sums = third_phase(*sums, [project.shape[1] for _, project in weights])
    results = [value for pair in sums for value in pair]
    return (sent.reshape(student.shape[0], 16, -1), *results)


def shards(
    student,
    dino_target,
    siglip_target,
    clip_target,
    image_owner,
    patch_count,
    dino_expand,
    dino_project,
    siglip_expand,
    siglip_project,
    clip_expand,
    clip_project,
):
    store = (lax.axis_index("y") * 4 + lax.axis_index("z")) * 2 + lax.axis_index("xh")
    per_store = dino_target.shape[0]
    owners = lax.dynamic_slice_in_dim(image_owner[:, 0], store * per_store, per_store)
    counts = lax.dynamic_slice_in_dim(patch_count, store * per_store, per_store)
    loss_scale = 1.0 / jnp.sqrt(jnp.sum(patch_count).astype(jnp.float32))
    weights = (
        (dino_expand, dino_project),
        (siglip_expand, siglip_project),
        (clip_expand, clip_project),
    )
    return step(
        student, (dino_target, siglip_target, clip_target), owners, counts, loss_scale, weights, 512
    )


def solution(mesh):
    fine = Mesh(mesh.devices.reshape(SIZES), DP + MP)
    return jax.shard_map(
        shards,
        mesh=fine,
        in_specs=(
            P(DP, None, None),
            P(DP, None, MP),
            P(DP, None, MP),
            P(DP, None, MP),
            P(),
            P(),
            P(None, MP),
            P(MP, None),
            P(None, MP),
            P(MP, None),
            P(None, MP),
            P(MP, None),
        ),
        out_specs=(
            P(DP, None, MP),
            P(DP, MP),
            P(MP, DP),
            P(DP, MP),
            P(MP, DP),
            P(DP, MP),
            P(MP, DP),
        ),
        check_vma=False,
    )
```

```python
import jax
import jax.numpy as jnp
from jax import lax
from jax.sharding import Mesh
from jax.sharding import PartitionSpec as P

DP = ("y", "z", "xh")
MP = ("xl", "core")
SIZES = (4, 4, 2, 2, 2)


def gelu_parts(hidden):
    normal_cdf = 0.5 * (1.0 + jax.scipy.special.erf(hidden * 0.7071067811865476))
    density = jnp.exp(-0.5 * hidden * hidden) * 0.3989422804014327
    return (hidden * normal_cdf, normal_cdf + hidden * density)


def swap(value, axis):
    return lax.ppermute(value, axis, [(0, 1), (1, 0)])


def mm(a, b, dims):
    return lax.dot_general(a, b, (dims, ((), ())), preferred_element_type=jnp.float32)


def row_plan(owners, counts, rows, core):
    images, patches = owners.shape[0], 16
    index = jnp.arange(images, dtype=jnp.int32)
    earlier = index[None, :] < index[:, None]
    rank = jnp.sum(((owners[:, None] == owners[None, :]) & earlier).astype(jnp.int32), axis=1)
    start = jnp.sum(jnp.where(earlier, counts[None, :], 0), axis=1)
    patch = jnp.arange(patches, dtype=jnp.int32)
    live = patch[None, :] < counts[:, None]
    number = start[:, None] + patch[None, :]
    half = rows // 2
    upper = (number >= half).astype(jnp.int32)
    place = number - upper * half + (upper ^ core ^ 1) * half
    place = jnp.where(live, place, -1).reshape(-1)
    source = ((rank ^ core)[:, None] * 32 + owners[:, None]) * patches + patch[None, :]
    source = jnp.where(live, source, -1).reshape(-1)
    here = place[None, :] == jnp.arange(rows, dtype=jnp.int32)[:, None]
    origin = jnp.sum(jnp.where(here, source[None, :] + 1, 0), axis=1) - 1
    total = 2 * 32 * patches
    from_slots = origin[:, None] == jnp.arange(total, dtype=jnp.int32)[None, :]
    return here.astype(jnp.bfloat16), from_slots.astype(jnp.bfloat16)


def after(value, *others):
    return lax.optimization_barrier((value, others))[0]


def ring_cuts(parts, axis, dim, flip=0):
    here = lax.axis_index(axis)

    def cut(ahead):
        index = ((here + ahead) % 4) ^ flip
        cuts = [lax.dynamic_index_in_dim(value, index, dim, keepdims=False) for value in parts]
        return cuts[0] if len(cuts) == 1 else jnp.concatenate(cuts, axis=-2)

    return [cut(ahead) for ahead in range(4)]


def ring_send(cuts, axis):
    return [cuts[0]] + [
        lax.ppermute(cuts[ahead], axis, [(i, (i + ahead) % 4) for i in range(4)])
        for ahead in (1, 3, 2)
    ]


def ring_add(arrived):
    total = arrived[0].astype(jnp.float32)
    for value in arrived[1:]:
        total = total + value.astype(jnp.float32)
    return total.astype(jnp.bfloat16)


def ring_ask(parts, axis, dim, flip=0):
    chunks = ring_cuts(parts, axis, dim, flip)
    return chunks, (chunks[2][:2], chunks[2][2:])


def ring_first(halves, axis):
    ahead, behind = [(i, (i + 1) % 4) for i in range(4)], [(i, (i + 3) % 4) for i in range(4)]
    return lax.ppermute(halves[0], axis, ahead), lax.ppermute(halves[1], axis, behind)


def ring_next(chunks, arrived):
    up = chunks[1][:2].astype(jnp.float32) + arrived[0].astype(jnp.float32)
    down = chunks[3][2:].astype(jnp.float32) + arrived[1].astype(jnp.float32)
    return (
        jnp.concatenate([up.astype(jnp.bfloat16), chunks[1][2:]], axis=0),
        jnp.concatenate([chunks[3][:2], down.astype(jnp.bfloat16)], axis=0),
    )


def second_phase(expand, project):
    expand = ring_cuts([expand], "y", 0)
    project = ring_cuts([project], "z", 0)
    return ring_add(ring_send(expand, "y")), ring_add(ring_send(project, "z"))


def third_phase(expand, project, widths):
    xh = lax.axis_index("xh")

    def add(low, high):
        got = swap(jnp.where(xh == 0, high, low), "xh")
        return jnp.where(xh == 0, low, high).astype(jnp.float32) + got.astype(jnp.float32)

    at, cuts = 0, []
    for width in widths:
        cuts.append(project[at : at + width // 16])
        at += width // 16
    low = jnp.concatenate([cut[: cut.shape[0] // 2] for cut in cuts], axis=0)
    high = jnp.concatenate([cut[cut.shape[0] // 2 :] for cut in cuts], axis=0)
    second = add(low, high)
    first = add(expand[:40], expand[40:])
    at, outs = 0, []
    for i, width in enumerate(widths):
        rows = width // 32
        outs.append((first[:, 384 * i : 384 * (i + 1)], second[at : at + rows].T))
        at += rows
    return outs


def step(student, targets, owners, counts, loss_scale, weights, rows):
    core, xl = lax.axis_index("core"), lax.axis_index("xl")
    half = rows // 2

    slots = student.reshape(32, 2, 16, -1)
    mine = lax.dynamic_index_in_dim(slots, core, 1, keepdims=False)
    mine = lax.all_to_all(mine, DP, split_axis=0, concat_axis=0, tiled=True)
    mine = mine.reshape(32 * 16, -1)

    def halves(project):
        cut = project.shape[1] // 2
        low, high = project[:, :cut], project[:, cut:]
        return jnp.where(xl == 0, low, high), jnp.where(xl == 0, high, low)
    expands = jnp.concatenate([expand for expand, _ in weights], axis=1)
    cuts = [halves(project) for _, project in weights]
    to_rows, from_slots = row_plan(owners, counts, rows, core)
    mine = after(mine, expands, cuts, from_slots)
    other = swap(mine, "core")
    x = (
        mm(from_slots[:, :512], mine, ((1,), (0,))) + mm(from_slots[:, 512:], other, ((1,), (0,)))
    ).astype(jnp.bfloat16)

    act_all, slope_all = gelu_parts(mm(x, expands, ((1,), (0,))))
    act_all = act_all.astype(jnp.bfloat16)
    acts = [act_all[:, 384 * i : 384 * (i + 1)] for i in range(3)]

    far_sums, nears = [], []
    for i, (own_cut, far_cut) in enumerate(cuts):
        if i > 0:
            acts[i] = after(acts[i], far_sums[-1])
        act = acts[i]
        near_far = swap(mm(act[:half], far_cut, ((1,), (0,))).astype(jnp.bfloat16), "core")
        nears.append(swap(mm(act[:half], own_cut, ((1,), (0,))).astype(jnp.bfloat16), "core"))
        far_sum = mm(act[half:], far_cut, ((1,), (0,))) + near_far.astype(jnp.float32)
        far_sums.append(far_sum.astype(jnp.bfloat16))
    targets = after(targets, far_sums[0])

    wanted = []
    for target in targets:
        flat = target.reshape(512, -1)
        sent = mm(to_rows[:half], flat, ((1,), (0,))).astype(jnp.bfloat16)
        kept = mm(to_rows[half:], flat, ((1,), (0,))).astype(jnp.bfloat16)
        got = swap(sent, "core")
        wanted.append(
            jnp.concatenate([jnp.where(core == 0, kept, got), jnp.where(core == 0, got, kept)], axis=1)
        )

    owns = []
    for (own_cut, _), act, near_own, target in zip(cuts, acts, nears, wanted):
        own = mm(after(act[half:], far_sums[2]), own_cut, ((1,), (0,)))
        owns.append((own + near_own.astype(jnp.float32)) - target.astype(jnp.float32))
    by_xl, by_core, residuals = [], [], []
    for i, (own, far_sum) in enumerate(zip(owns, far_sums)):
        if i > 0:
            own = after(own, residuals[-1])
        residual = (own + swap(far_sum, "xl").astype(jnp.float32)).astype(jnp.bfloat16)
        residuals.append(residual)
        by_xl.append(swap(residual, "xl"))
        by_core.append(swap(residual, "core"))

    flip = xl * 2
    blocks, project_grads = [], []
    for i in range(3):
        act = act_all[:, 384 * i : 384 * (i + 1)]
        near = jnp.concatenate([by_core[i], residuals[i]], axis=0)
        far = jnp.concatenate([swap(by_xl[i], "core"), by_xl[i]], axis=0)
        blocks.append((near, far))
        parts = [mm(part, act, ((0,), (0,))) * loss_scale for part in (near, far)]
        project_grads.append(jnp.concatenate([p.astype(jnp.bfloat16) for p in parts], axis=0))
    project_chunks, project_halves = ring_ask(
        [p.reshape(4, 4, -1, 384) for p in project_grads], "y", 0, flip
    )
    project_came = ring_first(project_halves, "y")
    blocks = after(blocks, project_halves)
    backs = [
        mm(near, own_cut, ((1,), (1,))) + mm(far, far_cut, ((1,), (1,)))
        for (near, far), (own_cut, far_cut) in zip(blocks, cuts)
    ]
    hidden_grad = (jnp.concatenate(backs, axis=1) * slope_all).astype(jnp.bfloat16)
    expand_grad = (mm(x, hidden_grad, ((0,), (0,))) * loss_scale).astype(jnp.bfloat16)
    expand_chunks, expand_halves = ring_ask([expand_grad.reshape(4, 4, 80, -1)], "z", 1)
    expand_came = ring_first(expand_halves, "z")
    hidden_grad = after(hidden_grad, expand_halves)

    def columns(xl_of, core_of):
        part = lax.dynamic_slice_in_dim(expands, (xl_of * 2 + core_of) * 320, 320, 0)
        return mm(hidden_grad, part, ((1,), (1,)))

    def core_order(value):
        return jnp.concatenate([value[half:], value[:half]], axis=0).astype(jnp.float32)

    near_far = columns(1 - xl, 1 - core).astype(jnp.bfloat16)
    near_own = columns(xl, 1 - core).astype(jnp.bfloat16)
    near_far, near_own = swap(near_far, "core"), swap(near_own, "core")
    far_sum = (columns(1 - xl, core) + core_order(near_far)).astype(jnp.bfloat16)
    far = swap(far_sum, "xl")
    project_next = ring_next(after(project_chunks, far_sum), project_came)
    expand_next = ring_next(after(expand_chunks, far_sum), expand_came)
    project_sums = ring_first(project_next, "y")
    expand_sums = ring_first(expand_next, "z")
    own = columns(xl, core) + core_order(near_own)
    grad = (own + far.astype(jnp.float32)).astype(jnp.bfloat16)
    placed = mm(from_slots, grad, ((0,), (0,))).astype(jnp.bfloat16).reshape(2, 32, 16, -1)
    placed = jnp.where(core == 0, placed, placed[::-1]).transpose(1, 0, 2, 3)
    sent = lax.all_to_all(placed, DP, split_axis=0, concat_axis=0, tiled=True)
    sums = second_phase(
        ring_add([after(expand_chunks[0], placed), *expand_sums]),
        ring_add([after(project_chunks[0], placed), *project_sums]),
    )
    sums = (after(sums[0], sent), sums[1])
    sums = third_phase(*sums, [project.shape[1] for _, project in weights])
    results = [value for pair in sums for value in pair]
    return (sent.reshape(student.shape[0], 16, -1), *results)


def shards(
    student,
    dino_target,
    siglip_target,
    clip_target,
    image_owner,
    patch_count,
    dino_expand,
    dino_project,
    siglip_expand,
    siglip_project,
    clip_expand,
    clip_project,
):
    store = (lax.axis_index("y") * 4 + lax.axis_index("z")) * 2 + lax.axis_index("xh")
    per_store = dino_target.shape[0]
    owners = lax.dynamic_slice_in_dim(image_owner[:, 0], store * per_store, per_store)
    counts = lax.dynamic_slice_in_dim(patch_count, store * per_store, per_store)
    loss_scale = 1.0 / jnp.sqrt(jnp.sum(patch_count).astype(jnp.float32))
    weights = (
        (dino_expand, dino_project),
        (siglip_expand, siglip_project),
        (clip_expand, clip_project),
    )
    return step(
        student, (dino_target, siglip_target, clip_target), owners, counts, loss_scale, weights, 512
    )


def solution(mesh):
    fine = Mesh(mesh.devices.reshape(SIZES), DP + MP)
    return jax.shard_map(
        shards,
        mesh=fine,
        in_specs=(
            P(DP, None, None),
            P(DP, None, MP),
            P(DP, None, MP),
            P(DP, None, MP),
            P(),
            P(),
            P(None, MP),
            P(MP, None),
            P(None, MP),
            P(MP, None),
            P(None, MP),
            P(MP, None),
        ),
        out_specs=(
            P(DP, None, MP),
            P(DP, MP),
            P(MP, DP),
            P(DP, MP),
            P(MP, DP),
            P(DP, MP),
            P(MP, DP),
        ),
        check_vma=False,
    )
```
